32 devices in a mesh: rep: 2 (over y), ep: 4 (over z), dp: 4 (over x, core).
Axes of the slice: x: 2, y: 2, z: 4, core: 2. Of those that a mesh axis runs over, the one named last changes fastest.
Arguments:
- tokens: bfloat16 [256, 4096], P(('rep', 'ep', 'dp')), parts along dimension 0, may hold values from -6 to 6
- expert_ids: int32 [256, 8], P(('rep', 'ep', 'dp')), parts along dimension 0, may hold values from 0 to 63, all different within a row; in each aligned block of 8 rows (0 to 7, 8 to 15, ...) at most 2 rows name the same one
- gate_scores: float32 [256, 8], P(('rep', 'ep', 'dp')), parts along dimension 0, may hold values from 0.05 to 1
- gate_weight: bfloat16 [64, 4096, 768], P('ep', None, 'dp'), may hold values from -0.09375 to 0.09375
- up_weight: bfloat16 [64, 4096, 768], P('ep', None, 'dp'), may hold values from -0.09375 to 0.09375
- down_weight: bfloat16 [64, 768, 4096], P('ep', 'dp'), may hold values from -0.21875 to 0.21875
Outputs:
- moe_output: bfloat16 [256, 4096], P(('rep', 'ep', 'dp')), parts along dimension 0
The draws below stay inside these ranges and needn't reach their ends.
There are 2 independent parts, one for each index of `rep`. The reference program is written for one: setup_inputs(seed, part) draws one part's arguments, and reference() takes and returns one part's arrays. A program takes and returns all parts, laid end to end along the dimension named above; an argument that names none is the same for every part. Nothing has to cross between parts.
Inputs may be any that keep to these rules, and one draw needn't show every extreme that they name: `expert_ids`: the 8 ids of a token are distinct. Among the 8 tokens of one device no expert is named by more than 2 tokens, and in every draw some device names some expert exactly 2 times.
All inputs are finite; a program needn't handle non-finite values.
Results may differ from the reference program's by a relative error of at most 0.011.
Values may be sent and summed in bfloat16 or wider, within the bound.
No kernel may reach another device: no remote copies, remote signals or barrier semaphores. Data moves between devices by JAX's collectives and lax.ppermute only.
A program may use at most 192 MiB of HBM per device.

```python
import math
import jax
import jax.numpy as jnp
import numpy as np
from jax import lax

D = 4096
FF = 768
EXPERTS = 64
TOP = 8
TOK_DEV = 8
CAP = 2
TOKENS = 128
N_EP = 4
N_DP = 4


def shard_levels(stream_key, shape, cuts, low, largest):
    def one(dim, parts):
        heights = jax.random.uniform(jax.random.fold_in(jax.random.fold_in(stream_key, 6), dim), (parts,), jnp.float32, low / len(cuts), largest / len(cuts))
        return jnp.repeat(jnp.exp(heights), shape[dim] // parts).reshape((-1,) + (1,) * (len(shape) - dim - 1))

    factor_of = one(*cuts[0])
    for cut in cuts[1:]:
        factor_of = factor_of * one(*cut)
    return factor_of


def routed_block(own_key, own, number, rows, count, top, bound, skew):
    ranking = jax.random.permutation(own_key, count)
    crowded, ordinary = portions_of(count, rows * top, bound, skew, True), portions_of(count, rows * top, bound, skew, False)
    places = jnp.arange(count)

    def named(tallies, rotation):
        used = int((tallies > 0).sum())
        fixed = max(1, used // 4)
        shifted = fixed + (places - fixed + rotation * (used - fixed)) % max(1, count - fixed)
        return jnp.zeros((count,), jnp.int32).at[ranking[jnp.where(places < fixed, places, shifted)]].set(jnp.asarray(tallies, jnp.int32))

    tallies = jnp.where(number % 4 == 0, named(crowded, number // 4), named(ordinary, number - number // 4 - 1))
    mixed = jax.random.permutation(jax.random.fold_in(own, 3), count)
    giver, receiver = mixed[0:count // 2 * 2:2], mixed[1:count // 2 * 2:2]
    margin = jnp.minimum(tallies[giver] - 1, bound - tallies[receiver]) // 2
    margin = jnp.where((giver == ranking[0]) | (receiver == ranking[0]) | (tallies[receiver] == 0), 0, jnp.maximum(margin, 0))
    shifted = jax.random.randint(jax.random.fold_in(own, 4), (count // 2,), 0, 1 << 20) % (margin + 1)
    tallies = tallies.at[giver].add(-shifted).at[receiver].add(shifted)
    labels = jnp.searchsorted(jnp.cumsum(tallies), jnp.arange(rows * top), side="right").astype(jnp.int32)
    grid = labels.reshape(top, rows).T
    grid = grid[jax.random.permutation(jax.random.fold_in(own, 1), rows)]
    rotation = jax.random.randint(jax.random.fold_in(own, 2), (rows, 1), 0, top)
    return jnp.take_along_axis(grid, (jnp.arange(top)[None, :] + rotation) % top, axis=1)


def portions_of(amount, total, limit, slope, full):
    loads = [(1 << 20) // math.isqrt(rank ** slope) + 1 for rank in range(1, amount + 1)]
    largest = limit if full else min(limit, max(-(-total // amount), total * loads[0] // sum(loads)))
    least = 1 if total - largest >= amount - 1 else 0
    given, spare = [largest] + [least] * (amount - 1), total - largest - least * (amount - 1)
    while spare > 0:
        movable = [i for i in range(1, amount) if given[i] < largest] or [i for i in range(1, amount) if given[i] < limit]
        mass, budget = sum([loads[i] for i in movable]), spare
        for i in movable:
            addition = min(limit - given[i], max(1, budget * loads[i] // mass), spare)
            given[i] = given[i] + addition
            spare = spare - addition
    return np.array(given)


def gaussian(rng, dims, deviation, most, pieces=(), held_as=jnp.bfloat16):
    values = deviation * jax.random.normal(rng, dims, jnp.float32)
    if pieces:
        values = values * shard_levels(rng, dims, pieces, -0.22, 0.18)
    return jnp.clip(values, -most, most).astype(held_as)


def setup_inputs(seed: int = 0, part: int = 0) -> dict:
    keys = jax.random.split(jax.random.key(seed), 7)
    own_keys = jax.random.split(jax.random.fold_in(keys[6], part), 7)
    tokens = gaussian(own_keys[0], (TOKENS, D), 1.0, 6.0, ((0, 16),))
    expert_ids_keys = jax.random.split(jax.random.fold_in(own_keys[1], 1), TOKENS // TOK_DEV)
    expert_ids_turns = jax.random.permutation(jax.random.fold_in(own_keys[1], 3), TOKENS // TOK_DEV)
    expert_ids = jax.vmap(lambda own, number: routed_block(jax.random.fold_in(own_keys[1], 2), own, number, TOK_DEV, EXPERTS, TOP, CAP, 2))(expert_ids_keys, expert_ids_turns).reshape((TOKENS, TOP))
    gate_scores = jnp.clip(jnp.exp(math.log(1.0) - 2.9957323 * jax.random.uniform(own_keys[2], (TOKENS, TOP), jnp.float32) ** shard_levels(own_keys[2], (TOKENS, TOP), ((0, 16),), -0.2, 0.2)), 0.05, 1.0)
    gate_weight = gaussian(keys[3], (EXPERTS, D, FF), D ** -0.5, 0.09375, ((0, 4), (2, 4)))
    up_weight = gaussian(keys[4], (EXPERTS, D, FF), D ** -0.5, 0.09375, ((0, 4), (2, 4)))
    down_weight = gaussian(keys[5], (EXPERTS, FF, D), FF ** -0.5, 0.21875, ((0, 4), (1, 4)))
    return dict(tokens=tokens, expert_ids=expert_ids, gate_scores=gate_scores, gate_weight=gate_weight, up_weight=up_weight, down_weight=down_weight)


def reference(tokens, expert_ids, gate_scores, gate_weight, up_weight, down_weight):
    token_count = tokens.shape[0]
    flat_ids = expert_ids.reshape(-1).astype(jnp.int32)
    weights = gate_scores / jnp.sum(gate_scores, axis=1, keepdims=True)
    flat_weights = weights.reshape(-1)
    token_owner = (jnp.arange(token_count * TOP, dtype=jnp.int32) // TOP).astype(jnp.int32)
    most_rows = N_EP * N_DP * CAP
    block_width = FF // N_DP

    def one_expert(running, expert):
        picked = flat_ids == expert
        row_index = jnp.nonzero(picked, size=most_rows, fill_value=0)[0].astype(jnp.int32)
        is_valid = (jnp.arange(most_rows, dtype=jnp.int32) < jnp.sum(picked.astype(jnp.int32))).astype(jnp.float32)
        owners = token_owner[row_index]
        picked_rows = tokens[owners]
        gate_acts = jnp.dot(picked_rows, gate_weight[expert], preferred_element_type=jnp.float32)
        up_acts = jnp.dot(picked_rows, up_weight[expert], preferred_element_type=jnp.float32)
        hidden = (jax.nn.silu(gate_acts) * up_acts).astype(jnp.bfloat16)
        slice_parts = jnp.einsum(
            "rjf,jfd->rjd",
            hidden.reshape(most_rows, N_DP, block_width).astype(jnp.float32),
            down_weight[expert].reshape(N_DP, block_width, D).astype(jnp.float32),
        )
        slice_parts = lax.optimization_barrier(slice_parts.astype(jnp.bfloat16)).astype(jnp.float32)
        expert_out = jnp.sum(slice_parts, axis=1).astype(jnp.bfloat16)
        contribution = expert_out.astype(jnp.float32) * (flat_weights[row_index] * is_valid)[:, None]
        running = running.at[owners].add(contribution)
        return running, None

    accumulated, _ = lax.scan(one_expert, jnp.zeros((token_count, D), jnp.float32), jnp.arange(EXPERTS, dtype=jnp.int32))
    return accumulated.astype(jnp.bfloat16)
```

```python
import functools

import jax
import jax.numpy as jnp
from jax import lax
from jax.experimental import pallas as pl
from jax.experimental.pallas import tpu as pltpu
from jax.sharding import PartitionSpec as P

BF16 = jnp.bfloat16
F32 = jnp.float32
NT = (((1,), (1,)), ((), ()))


def add_up(*parts):
    total = parts[0].astype(F32)
    for part in parts[1:]:
        total = total + part.astype(F32)
    return total.astype(BF16)


def hop(x, ep_count, dp_count, ep_mask, dp_mask):
    pairs = [
        (i, ((i // dp_count) ^ ep_mask) * dp_count + ((i % dp_count) ^ dp_mask))
        for i in range(ep_count * dp_count)
    ]
    return lax.ppermute(x, ("ep", "dp"), pairs)


def ep_order(ep_count):
    return sorted(range(1, ep_count), key=lambda m: (-m.bit_length(), m))


def gather_rows(x, ep_count, dp_count):
    send = functools.partial(hop, ep_count=ep_count, dp_count=dp_count)
    blocks = {(0, 0): x}
    for m in ep_order(ep_count):
        blocks[m, 0] = send(x, ep_mask=m, dp_mask=0)
    for d in range(2, dp_count, 2):
        for m in [0] + ep_order(ep_count):
            blocks[m, d] = send(blocks[m, 0], ep_mask=0, dp_mask=d)
    near = jnp.concatenate(
        [blocks[m, d] for d in range(0, dp_count, 2) for m in range(ep_count)], axis=0
    )
    return jnp.concatenate([near, send(near, ep_mask=0, dp_mask=1)], axis=0)


def scatter_rows(y, ep_count, dp_count):
    send = functools.partial(hop, ep_count=ep_count, dp_count=dp_count)
    rows = y.shape[0]
    y = y.reshape(2, dp_count // 2, ep_count, rows // (ep_count * dp_count), y.shape[1])
    y = add_up(y[0], send(y[1], ep_mask=0, dp_mask=1))
    y = add_up(y[0], *[send(y[d // 2], ep_mask=0, dp_mask=d) for d in range(2, dp_count, 2)])
    return add_up(y[0], *[send(y[m], ep_mask=m, dp_mask=0) for m in ep_order(ep_count)])


def hidden_kernel(width, expert_total, first_ref, x_ref, gate_ref, up_ref, h_ref):
    model_width = gate_ref.shape[1]
    step = gate_ref.shape[0]
    x = x_ref[:, :model_width]
    gate_acts = lax.dot_general(x, gate_ref[...], NT, preferred_element_type=F32)
    up_acts = lax.dot_general(x, up_ref[...], NT, preferred_element_type=F32)
    shape = (x_ref.shape[1] - model_width, step)
    row = lax.broadcasted_iota(jnp.int32, shape, 0)
    column = lax.broadcasted_iota(jnp.int32, shape, 1)
    expert = first_ref[0] + pl.program_id(0) * (step // width) + column // width
    spread = (lax.rem(row, expert_total) == expert).astype(F32).astype(BF16)
    weight = jnp.dot(x_ref[:, model_width:], spread, preferred_element_type=F32)
    h_ref[...] = (jax.nn.silu(gate_acts) * up_acts * weight).astype(BF16)


def down_kernel(h_ref, down_ref, y_ref):
    y_ref[...] = jnp.dot(h_ref[...], down_ref[...], preferred_element_type=F32).astype(BF16)


def experts(rows, gate, up, down, first, width, expert_total):
    token_count = rows.shape[0]
    units, model_width = gate.shape
    step = 2 * width if units % (2 * width) == 0 else width
    hidden = pl.pallas_call(
        functools.partial(hidden_kernel, width, expert_total),
        grid=(units // step,),
        in_specs=[
            pl.BlockSpec(memory_space=pltpu.SMEM),
            pl.BlockSpec(rows.shape, lambda i: (0, 0)),
            pl.BlockSpec((step, model_width), lambda i: (i, 0)),
            pl.BlockSpec((step, model_width), lambda i: (i, 0)),
        ],
        out_specs=pl.BlockSpec((token_count, step), lambda i: (0, i)),
        out_shape=jax.ShapeDtypeStruct((token_count, units), BF16),
        compiler_params=pltpu.CompilerParams(vmem_limit_bytes=32 << 20),
        name="hidden",
    )(first, rows, gate, up)
    piece = 512
    return pl.pallas_call(
        down_kernel,
        grid=(model_width // piece,),
        in_specs=[
            pl.BlockSpec((token_count, units), lambda i: (0, 0)),
            pl.BlockSpec((units, piece), lambda i: (0, i)),
        ],
        out_specs=pl.BlockSpec((token_count, piece), lambda i: (0, i)),
        out_shape=jax.ShapeDtypeStruct((token_count, model_width), BF16),
        compiler_params=pltpu.CompilerParams(vmem_limit_bytes=32 << 20),
        name="down",
    )(hidden, down)


def experts_plain(rows, gate, up, down, first, width, expert_total):
    units, model_width = gate.shape
    x = rows[:, :model_width]
    gate_acts = lax.dot_general(x, gate, NT, preferred_element_type=F32)
    up_acts = lax.dot_general(x, up, NT, preferred_element_type=F32)
    row = jnp.arange(rows.shape[1] - model_width, dtype=jnp.int32)[:, None]
    expert = first[0] + jnp.arange(units, dtype=jnp.int32)[None, :] // width
    spread = (row % expert_total == expert).astype(BF16)
    weight = jnp.dot(rows[:, model_width:], spread, preferred_element_type=F32)
    hidden = (jax.nn.silu(gate_acts) * up_acts * weight).astype(BF16)
    return jnp.dot(hidden, down, preferred_element_type=F32).astype(BF16)


def local(tokens, expert_ids, gate_scores, gate_weight, up_weight, down_weight):
    model_width = tokens.shape[1]
    ep_count = lax.axis_size("ep")
    dp_count = lax.axis_size("dp")
    local_experts, _, width = gate_weight.shape
    expert_total = local_experts * ep_count
    gate = jnp.swapaxes(gate_weight, 1, 2).reshape(local_experts * width, model_width)
    up = jnp.swapaxes(up_weight, 1, 2).reshape(local_experts * width, model_width)
    down = down_weight.reshape(local_experts * width, model_width)
    first = (lax.axis_index("ep") * local_experts).astype(jnp.int32).reshape(1)

    weights = gate_scores / jnp.sum(gate_scores, axis=1, keepdims=True)
    named = expert_ids[:, :, None] == jnp.arange(expert_total, dtype=jnp.int32)[None, None, :]
    dense = jnp.sum(jnp.where(named, weights[:, :, None], 0.0), axis=1)
    high = lax.reduce_precision(dense, 8, 7)
    message = jnp.concatenate([tokens, high.astype(BF16), (dense - high).astype(BF16)], axis=1)

    powers = all(n & (n - 1) == 0 for n in (ep_count, dp_count))
    if powers and ep_count <= 8 and 2 <= dp_count <= 8:
        rows = gather_rows(message, ep_count, dp_count)
        partial = experts(rows, gate, up, down, first, width, expert_total)
        return scatter_rows(partial, ep_count, dp_count)
    rows = lax.all_gather(message, ("ep", "dp"), axis=0, tiled=True)
    partial = experts_plain(rows, gate, up, down, first, width, expert_total)
    return lax.psum_scatter(partial, ("ep", "dp"), scatter_dimension=0, tiled=True)


def solution(mesh):
    in_specs = (
        P(("rep", "ep", "dp"), None),
        P(("rep", "ep", "dp"), None),
        P(("rep", "ep", "dp"), None),
        P("ep", None, "dp"),
        P("ep", None, "dp"),
        P("ep", "dp", None),
    )
    out_specs = P(("rep", "ep", "dp"), None)
    return jax.shard_map(local, mesh=mesh, in_specs=in_specs, out_specs=out_specs, check_vma=False)
```

```python
import functools

import jax
import jax.numpy as jnp
from jax import lax
from jax.experimental import pallas as pl
from jax.experimental.pallas import tpu as pltpu
from jax.sharding import PartitionSpec as P

BF16 = jnp.bfloat16
F32 = jnp.float32
NT = (((1,), (1,)), ((), ()))


def add_up(*parts):
    total = parts[0].astype(F32)
    for part in parts[1:]:
        total = total + part.astype(F32)
    return total.astype(BF16)


def hop(x, ep_count, dp_count, ep_mask, dp_mask):
    pairs = [
        (i, ((i // dp_count) ^ ep_mask) * dp_count + ((i % dp_count) ^ dp_mask))
        for i in range(ep_count * dp_count)
    ]
    return lax.ppermute(x, ("ep", "dp"), pairs)


def ep_order(ep_count):
    return sorted(range(1, ep_count), key=lambda m: (-m.bit_length(), m))


def gather_rows(x, ep_count, dp_count):
    send = functools.partial(hop, ep_count=ep_count, dp_count=dp_count)
    blocks = {(0, 0): x}
    for m in ep_order(ep_count):
        blocks[m, 0] = send(x, ep_mask=m, dp_mask=0)
    for d in range(2, dp_count, 2):
        for m in [0] + ep_order(ep_count):
            blocks[m, d] = send(blocks[m, 0], ep_mask=0, dp_mask=d)
    near = jnp.concatenate(
        [blocks[m, d] for d in range(0, dp_count, 2) for m in range(ep_count)], axis=0
    )
    return jnp.concatenate([near, send(near, ep_mask=0, dp_mask=1)], axis=0)


def scatter_rows(y, ep_count, dp_count):
    send = functools.partial(hop, ep_count=ep_count, dp_count=dp_count)
    rows = y.shape[0]
    y = y.reshape(2, dp_count // 2, ep_count, rows // (ep_count * dp_count), y.shape[1])
    y = add_up(y[0], send(y[1], ep_mask=0, dp_mask=1))
    y = add_up(y[0], *[send(y[d // 2], ep_mask=0, dp_mask=d) for d in range(2, dp_count, 2)])
    return add_up(y[0], *[send(y[m], ep_mask=m, dp_mask=0) for m in ep_order(ep_count)])


def experts_kernel(width, expert_total, step, piece, slots, down_slots,
                   first_ref, x_ref, gate_ref, up_ref, down_ref, y_ref,
                   h_ref, gate_buf, up_buf, down_buf, gate_sem, up_sem, down_sem):
    units, model_width = gate_ref.shape
    steps, pieces = units // step, model_width // piece

    def rows_copy(ref, buf, sem, i):
        return pltpu.make_async_copy(
            ref.at[pl.ds(i * step, step), :], buf.at[i % slots], sem.at[i % slots]
        )

    def gate_copy(i):
        return rows_copy(gate_ref, gate_buf, gate_sem, i)

    def up_copy(i):
        return rows_copy(up_ref, up_buf, up_sem, i)

    def down_copy(j):
        slot = j % down_slots
        return pltpu.make_async_copy(
            down_ref.at[:, pl.ds(j * piece, piece)], down_buf.at[slot], down_sem.at[slot]
        )

    for i in range(min(slots, steps)):
        gate_copy(i).start()
        up_copy(i).start()
    begun = 0
    for i in range(steps):
        x = x_ref[:, :model_width]
        rows = slice(i * step, (i + 1) * step)
        shape = (step, x_ref.shape[1] - model_width)
        expert = first_ref[0] + (lax.broadcasted_iota(jnp.int32, shape, 0) + i * step) // width
        column = lax.rem(lax.broadcasted_iota(jnp.int32, shape, 1), expert_total)
        spread = (column == expert).astype(F32).astype(BF16)
        weight = lax.dot_general(spread, x_ref[:, model_width:], NT, preferred_element_type=F32)
        gate_copy(i).wait()
        gate_acts = lax.dot_general(gate_buf[i % slots], x, NT, preferred_element_type=F32)
        gate_acts = jax.nn.silu(gate_acts) * weight
        up_copy(i).wait()
        up_acts = lax.dot_general(up_buf[i % slots], x, NT, preferred_element_type=F32)
        h_ref[:, rows] = (gate_acts * up_acts).T.astype(BF16)
        if i + slots < steps:
            gate_copy(i + slots).start()
            up_copy(i + slots).start()
        else:
            goal = min(pieces, down_slots) * (i + slots - steps + 1) // slots
            for j in range(begun, goal):
                down_copy(j).start()
            begun = max(begun, goal)
    for j in range(pieces):
        down_copy(j).wait()
        y_ref[:, j * piece : (j + 1) * piece] = jnp.dot(
            h_ref[...], down_buf[j % down_slots], preferred_element_type=F32
        ).astype(BF16)
        if j + down_slots < pieces:
            down_copy(j + down_slots).start()


def experts(rows, gate, up, down, first, width, expert_total):
    token_count = rows.shape[0]
    units, model_width = gate.shape
    step = 2 * width if units % (2 * width) == 0 else width
    piece, slots, down_slots = 512, 3, 6
    whole = pl.BlockSpec(memory_space=pltpu.VMEM)
    away = pl.BlockSpec(memory_space=pl.ANY)
    return pl.pallas_call(
        functools.partial(experts_kernel, width, expert_total, step, piece, slots, down_slots),
        in_specs=[pl.BlockSpec(memory_space=pltpu.SMEM), whole, away, away, away],
        out_specs=whole,
        out_shape=jax.ShapeDtypeStruct((token_count, model_width), BF16),
        scratch_shapes=[
            pltpu.VMEM((token_count, units), BF16),
            pltpu.VMEM((slots, step, model_width), BF16),
            pltpu.VMEM((slots, step, model_width), BF16),
            pltpu.VMEM((down_slots, units, piece), BF16),
            pltpu.SemaphoreType.DMA((slots,)),
            pltpu.SemaphoreType.DMA((slots,)),
            pltpu.SemaphoreType.DMA((down_slots,)),
        ],
        compiler_params=pltpu.CompilerParams(vmem_limit_bytes=44 << 20),
        name="experts",
    )(first, rows, gate, up, down)


def experts_plain(rows, gate, up, down, first, width, expert_total):
    units, model_width = gate.shape
    x = rows[:, :model_width]
    gate_acts = lax.dot_general(x, gate, NT, preferred_element_type=F32)
    up_acts = lax.dot_general(x, up, NT, preferred_element_type=F32)
    row = jnp.arange(rows.shape[1] - model_width, dtype=jnp.int32)[:, None]
    expert = first[0] + jnp.arange(units, dtype=jnp.int32)[None, :] // width
    spread = (row % expert_total == expert).astype(BF16)
    weight = jnp.dot(rows[:, model_width:], spread, preferred_element_type=F32)
    hidden = (jax.nn.silu(gate_acts) * up_acts * weight).astype(BF16)
    return jnp.dot(hidden, down, preferred_element_type=F32).astype(BF16)


def local(tokens, expert_ids, gate_scores, gate_weight, up_weight, down_weight):
    model_width = tokens.shape[1]
    ep_count = lax.axis_size("ep")
    dp_count = lax.axis_size("dp")
    local_experts, _, width = gate_weight.shape
    expert_total = local_experts * ep_count
    gate = jnp.swapaxes(gate_weight, 1, 2).reshape(local_experts * width, model_width)
    up = jnp.swapaxes(up_weight, 1, 2).reshape(local_experts * width, model_width)
    down = down_weight.reshape(local_experts * width, model_width)
    first = (lax.axis_index("ep") * local_experts).astype(jnp.int32).reshape(1)

    weights = gate_scores / jnp.sum(gate_scores, axis=1, keepdims=True)
    named = expert_ids[:, :, None] == jnp.arange(expert_total, dtype=jnp.int32)[None, None, :]
    dense = jnp.sum(jnp.where(named, weights[:, :, None], 0.0), axis=1)
    high = lax.reduce_precision(dense, 8, 7)
    message = jnp.concatenate([tokens, high.astype(BF16), (dense - high).astype(BF16)], axis=1)

    powers = all(n & (n - 1) == 0 for n in (ep_count, dp_count))
    if powers and ep_count <= 8 and 2 <= dp_count <= 8:
        rows = gather_rows(message, ep_count, dp_count)
        partial = experts(rows, gate, up, down, first, width, expert_total)
        return scatter_rows(partial, ep_count, dp_count)
    rows = lax.all_gather(message, ("ep", "dp"), axis=0, tiled=True)
    partial = experts_plain(rows, gate, up, down, first, width, expert_total)
    return lax.psum_scatter(partial, ("ep", "dp"), scatter_dimension=0, tiled=True)


def solution(mesh):
    in_specs = (
        P(("rep", "ep", "dp"), None),
        P(("rep", "ep", "dp"), None),
        P(("rep", "ep", "dp"), None),
        P("ep", None, "dp"),
        P("ep", None, "dp"),
        P("ep", "dp", None),
    )
    out_specs = P(("rep", "ep", "dp"), None)
    return jax.shard_map(local, mesh=mesh, in_specs=in_specs, out_specs=out_specs, check_vma=False)
```

```python
import functools

import jax
import jax.numpy as jnp
from jax import lax
from jax.experimental import pallas as pl
from jax.experimental.pallas import tpu as pltpu
from jax.sharding import PartitionSpec as P

BF16 = jnp.bfloat16
F32 = jnp.float32
NT = (((1,), (1,)), ((), ()))


def add_up(*parts):
    total = parts[0].astype(F32)
    for part in parts[1:]:
        total = total + part.astype(F32)
    return total.astype(BF16)


def hop(x, ep_count, dp_count, ep_mask, dp_mask):
    pairs = [
        (i, ((i // dp_count) ^ ep_mask) * dp_count + ((i % dp_count) ^ dp_mask))
        for i in range(ep_count * dp_count)
    ]
    return lax.ppermute(x, ("ep", "dp"), pairs)


def ep_order(ep_count):
    return sorted(range(1, ep_count), key=lambda m: (-m.bit_length(), m))


def gather_rows(x, ep_count, dp_count):
    send = functools.partial(hop, ep_count=ep_count, dp_count=dp_count)
    blocks = {(0, 0): x}
    for m in ep_order(ep_count):
        blocks[m, 0] = send(x, ep_mask=m, dp_mask=0)
    for d in range(2, dp_count, 2):
        for m in [0] + ep_order(ep_count):
            blocks[m, d] = send(blocks[m, 0], ep_mask=0, dp_mask=d)
    near = jnp.concatenate(
        [blocks[m, d] for d in range(0, dp_count, 2) for m in range(ep_count)], axis=0
    )
    return jnp.concatenate([near, send(near, ep_mask=0, dp_mask=1)], axis=0)


def scatter_rows(y, ep_count, dp_count):
    send = functools.partial(hop, ep_count=ep_count, dp_count=dp_count)
    rows = y.shape[0]
    y = y.reshape(2, dp_count // 2, ep_count, rows // (ep_count * dp_count), y.shape[1])
    y = add_up(y[0], send(y[1], ep_mask=0, dp_mask=1))
    y = add_up(y[0], *[send(y[d // 2], ep_mask=0, dp_mask=d) for d in range(2, dp_count, 2)])
    return add_up(y[0], *[send(y[m], ep_mask=m, dp_mask=0) for m in ep_order(ep_count)])


def message_kernel(expert_total, tokens_ref, ids_ref, scores_ref, out_ref):
    model_width = tokens_ref.shape[1]
    out_ref[:, :model_width] = tokens_ref[...]
    weights = scores_ref[...] / jnp.sum(scores_ref[...], axis=1, keepdims=True)
    shape = (tokens_ref.shape[0], 2 * expert_total)
    column = lax.broadcasted_iota(jnp.int32, shape, 1)
    dense = jnp.zeros(shape, F32)
    for k in range(ids_ref.shape[1]):
        named = ids_ref[:, k : k + 1] == lax.rem(column, expert_total)
        dense = dense + jnp.where(named, weights[:, k : k + 1], 0.0)
    high = dense.astype(BF16).astype(F32)
    out_ref[:, model_width:] = jnp.where(column < expert_total, high, dense - high).astype(BF16)


def message(tokens, expert_ids, gate_scores, expert_total):
    whole = pl.BlockSpec(memory_space=pltpu.VMEM)
    shape = (tokens.shape[0], tokens.shape[1] + 2 * expert_total)
    return pl.pallas_call(
        functools.partial(message_kernel, expert_total),
        in_specs=[whole] * 3,
        out_specs=whole,
        out_shape=jax.ShapeDtypeStruct(shape, BF16),
        compiler_params=pltpu.CompilerParams(vmem_limit_bytes=4 << 20),
        name="message",
    )(tokens, expert_ids, gate_scores)


def experts_kernel(width, expert_total, step, piece, slots, down_slots,
                   first_ref, x_ref, gate_ref, up_ref, down_ref, y_ref,
                   h_ref, buf, down_buf, sem, down_sem):
    units, model_width = gate_ref.shape
    steps, pieces = units // step, model_width // piece
    per_step = -(-down_slots // slots)

    def tile_copy(which, i):
        slot = lax.rem(i, slots)
        return pltpu.make_async_copy(
            (gate_ref, up_ref)[which].at[pl.ds(pl.multiple_of(i * step, step), step), :],
            buf.at[slot, pl.ds(which * step, step), :],
            sem.at[which, slot],
        )

    def down_copy(j):
        slot = lax.rem(j, down_slots)
        return pltpu.make_async_copy(
            down_ref.at[:, pl.ds(pl.multiple_of(j * piece, piece), piece)],
            down_buf.at[slot],
            down_sem.at[slot],
        )

    for i in range(slots):
        tile_copy(0, i).start()
        tile_copy(1, i).start()

    def hidden_step(i, carry):
        shape = (step, x_ref.shape[1] - model_width)
        expert = first_ref[0] + (lax.broadcasted_iota(jnp.int32, shape, 0) + i * step) // width
        column = lax.rem(lax.broadcasted_iota(jnp.int32, shape, 1), expert_total)
        spread = (column == expert).astype(F32).astype(BF16)
        weight = lax.dot_general(spread, x_ref[:, model_width:], NT, preferred_element_type=F32)
        tile_copy(0, i).wait()
        tile_copy(1, i).wait()
        acts = lax.dot_general(
            buf[lax.rem(i, slots)], x_ref[:, :model_width], NT, preferred_element_type=F32
        )
        hidden = jax.nn.silu(acts[:step]) * acts[step:] * weight
        h_ref[:, pl.ds(pl.multiple_of(i * step, step), step)] = hidden.T.astype(BF16)

        @pl.when(i + slots < steps)
        def _():
            tile_copy(0, i + slots).start()
            tile_copy(1, i + slots).start()

        @pl.when(i + slots >= steps)
        def _():
            for k in range(per_step):
                j = (i + slots - steps) * per_step + k

                @pl.when(j < down_slots)
                def _():
                    down_copy(j).start()

        return carry

    lax.fori_loop(0, steps, hidden_step, 0)

    def down_step(j, carry):
        down_copy(j).wait()
        y_ref[:, pl.ds(pl.multiple_of(j * piece, piece), piece)] = jnp.dot(
            h_ref[...], down_buf[lax.rem(j, down_slots)], preferred_element_type=F32
        ).astype(BF16)

        @pl.when(j + down_slots < pieces)
        def _():
            down_copy(j + down_slots).start()

        return carry

    lax.fori_loop(0, pieces, down_step, 0)


def experts(rows, gate, up, down, first, width, expert_total):
    token_count = rows.shape[0]
    units, model_width = gate.shape
    step, piece = 2 * width, 512
    slots, down_slots = min(3, units // step), min(6, model_width // piece)
    whole = pl.BlockSpec(memory_space=pltpu.VMEM)
    away = pl.BlockSpec(memory_space=pl.ANY)
    return pl.pallas_call(
        functools.partial(experts_kernel, width, expert_total, step, piece, slots, down_slots),
        in_specs=[pl.BlockSpec(memory_space=pltpu.SMEM), whole, away, away, away],
        out_specs=whole,
        out_shape=jax.ShapeDtypeStruct((token_count, model_width), BF16),
        scratch_shapes=[
            pltpu.VMEM((token_count, units), BF16),
            pltpu.VMEM((slots, 2 * step, model_width), BF16),
            pltpu.VMEM((down_slots, units, piece), BF16),
            pltpu.SemaphoreType.DMA((2, slots)),
            pltpu.SemaphoreType.DMA((down_slots,)),
        ],
        compiler_params=pltpu.CompilerParams(vmem_limit_bytes=44 << 20),
        name="experts",
    )(first, rows, gate, up, down)


def experts_plain(rows, gate, up, down, first, width, expert_total):
    units, model_width = gate.shape
    x = rows[:, :model_width]
    gate_acts = lax.dot_general(x, gate, NT, preferred_element_type=F32)
    up_acts = lax.dot_general(x, up, NT, preferred_element_type=F32)
    row = jnp.arange(rows.shape[1] - model_width, dtype=jnp.int32)[:, None]
    expert = first[0] + jnp.arange(units, dtype=jnp.int32)[None, :] // width
    spread = (row % expert_total == expert).astype(BF16)
    weight = jnp.dot(rows[:, model_width:], spread, preferred_element_type=F32)
    hidden = (jax.nn.silu(gate_acts) * up_acts * weight).astype(BF16)
    return jnp.dot(hidden, down, preferred_element_type=F32).astype(BF16)


def local(tokens, expert_ids, gate_scores, gate_weight, up_weight, down_weight):
    model_width = tokens.shape[1]
    ep_count = lax.axis_size("ep")
    dp_count = lax.axis_size("dp")
    local_experts, _, width = gate_weight.shape
    expert_total = local_experts * ep_count
    gate = jnp.swapaxes(gate_weight, 1, 2).reshape(local_experts * width, model_width)
    up = jnp.swapaxes(up_weight, 1, 2).reshape(local_experts * width, model_width)
    down = down_weight.reshape(local_experts * width, model_width)
    first = (lax.axis_index("ep") * local_experts).astype(jnp.int32).reshape(1)

    sent = message(tokens, expert_ids, gate_scores, expert_total)

    powers = all(n & (n - 1) == 0 for n in (ep_count, dp_count))
    if powers and ep_count <= 8 and 2 <= dp_count <= 8 and local_experts % 2 == 0:
        rows = gather_rows(sent, ep_count, dp_count)
        partial = experts(rows, gate, up, down, first, width, expert_total)
        return scatter_rows(partial, ep_count, dp_count)
    rows = lax.all_gather(sent, ("ep", "dp"), axis=0, tiled=True)
    partial = experts_plain(rows, gate, up, down, first, width, expert_total)
    return lax.psum_scatter(partial, ("ep", "dp"), scatter_dimension=0, tiled=True)


def solution(mesh):
    in_specs = (
        P(("rep", "ep", "dp"), None),
        P(("rep", "ep", "dp"), None),
        P(("rep", "ep", "dp"), None),
        P("ep", None, "dp"),
        P("ep", None, "dp"),
        P("ep", "dp", None),
    )
    out_specs = P(("rep", "ep", "dp"), None)
    return jax.shard_map(local, mesh=mesh, in_specs=in_specs, out_specs=out_specs, check_vma=False)
```

```python
import functools

import jax
import jax.numpy as jnp
from jax import lax
from jax.experimental import pallas as pl
from jax.experimental.pallas import tpu as pltpu
from jax.sharding import PartitionSpec as P

BF16 = jnp.bfloat16
F32 = jnp.float32
NT = (((1,), (1,)), ((), ()))


def add_up(*parts):
    total = parts[0].astype(F32)
    for part in parts[1:]:
        total = total + part.astype(F32)
    return total.astype(BF16)


def hop(x, ep_count, dp_count, ep_mask, dp_mask):
    pairs = [
        (i, ((i // dp_count) ^ ep_mask) * dp_count + ((i % dp_count) ^ dp_mask))
        for i in range(ep_count * dp_count)
    ]
    return lax.ppermute(x, ("ep", "dp"), pairs)


def ep_order(ep_count):
    return sorted(range(1, ep_count), key=lambda m: (-m.bit_length(), m))


def gather_rows(x, ep_count, dp_count):
    send = functools.partial(hop, ep_count=ep_count, dp_count=dp_count)
    blocks = {(0, 0): x}
    for m in ep_order(ep_count):
        blocks[m, 0] = send(x, ep_mask=m, dp_mask=0)
    for d in range(2, dp_count, 2):
        for m in [0] + ep_order(ep_count):
            blocks[m, d] = send(blocks[m, 0], ep_mask=0, dp_mask=d)
    near = jnp.concatenate(
        [blocks[m, d] for d in range(0, dp_count, 2) for m in range(ep_count)], axis=0
    )
    return jnp.concatenate([near, send(near, ep_mask=0, dp_mask=1)], axis=0)


def scatter_rows(y, ep_count, dp_count):
    send = functools.partial(hop, ep_count=ep_count, dp_count=dp_count)
    rows, half = y.shape[0], ep_count // 2
    y = y.reshape(2, dp_count // 2, ep_count, rows // (ep_count * dp_count), y.shape[1])
    y = add_up(y[0], send(y[1], ep_mask=0, dp_mask=1))
    others = range(2, dp_count, 2)
    far = [send(y[d // 2, half:], ep_mask=0, dp_mask=d) for d in others]
    near = [send(y[d // 2, :half], ep_mask=0, dp_mask=d) for d in others]
    far_sum = add_up(y[0, half:], *far)
    far_sent = [send(far_sum[m - half], ep_mask=m, dp_mask=0) for m in range(half, ep_count)]
    near, far_sent[0] = lax.optimization_barrier((near, far_sent[0]))
    near_sum = add_up(y[0, :half], *near)
    near_sent = [send(near_sum[m], ep_mask=m, dp_mask=0) for m in range(1, half)]
    return add_up(near_sum[0], *near_sent, *far_sent)


def message_kernel(expert_total, tokens_ref, ids_ref, scores_ref, out_ref, ids_buf, scores_buf, sem):
    model_width = tokens_ref.shape[1]
    copies = [
        pltpu.make_async_copy(ids_ref, ids_buf, sem.at[0]),
        pltpu.make_async_copy(scores_ref, scores_buf, sem.at[1]),
        pltpu.make_async_copy(tokens_ref, out_ref.at[:, pl.ds(0, model_width)], sem.at[2]),
    ]
    for copy in copies:
        copy.start()
    copies[0].wait()
    copies[1].wait()
    weights = scores_buf[...] / jnp.sum(scores_buf[...], axis=1, keepdims=True)
    shape = (tokens_ref.shape[0], 2 * expert_total)
    column = lax.broadcasted_iota(jnp.int32, shape, 1)
    dense = jnp.zeros(shape, F32)
    for k in range(ids_ref.shape[1]):
        named = ids_buf[:, k : k + 1] == lax.rem(column, expert_total)
        dense = dense + jnp.where(named, weights[:, k : k + 1], 0.0)
    high = dense.astype(BF16).astype(F32)
    out_ref[:, model_width:] = jnp.where(column < expert_total, high, dense - high).astype(BF16)
    copies[2].wait()


def message(tokens, expert_ids, gate_scores, expert_total):
    shape = (tokens.shape[0], tokens.shape[1] + 2 * expert_total)
    operands = (tokens, expert_ids, gate_scores)
    return pl.pallas_call(
        functools.partial(message_kernel, expert_total),
        in_specs=[pl.BlockSpec(memory_space=pltpu.HBM)] * 3,
        out_specs=pl.BlockSpec(memory_space=pltpu.VMEM),
        out_shape=jax.ShapeDtypeStruct(shape, BF16),
        scratch_shapes=[
            pltpu.VMEM(expert_ids.shape, jnp.int32),
            pltpu.VMEM(gate_scores.shape, F32),
            pltpu.SemaphoreType.DMA((3,)),
        ],
        compiler_params=pltpu.CompilerParams(vmem_limit_bytes=4 << 20),
        name="message",
    )(*[pltpu.with_memory_space_constraint(a, pltpu.HBM) for a in operands])


def experts_kernel(width, expert_total, step, piece, slots, down_slots,
                   first_ref, x_ref, gate_ref, up_ref, down_ref, y_ref,
                   h_ref, buf, down_buf, sem, down_sem):
    units, model_width = gate_ref.shape
    steps, pieces = units // step, model_width // piece
    per_step = -(-down_slots // slots)

    def tile_copy(which, i):
        slot = lax.rem(i, slots)
        return pltpu.make_async_copy(
            (gate_ref, up_ref)[which].at[pl.ds(pl.multiple_of(i * step, step), step), :],
            buf.at[slot, pl.ds(which * step, step), :],
            sem.at[which, slot],
        )

    def down_copy(j):
        slot = lax.rem(j, down_slots)
        return pltpu.make_async_copy(
            down_ref.at[:, pl.ds(pl.multiple_of(j * piece, piece), piece)],
            down_buf.at[slot],
            down_sem.at[slot],
        )

    for i in range(slots):
        tile_copy(0, i).start()
        tile_copy(1, i).start()

    def hidden_step(i, carry):
        shape = (step, x_ref.shape[1] - model_width)
        expert = first_ref[0] + (lax.broadcasted_iota(jnp.int32, shape, 0) + i * step) // width
        column = lax.rem(lax.broadcasted_iota(jnp.int32, shape, 1), expert_total)
        spread = (column == expert).astype(F32).astype(BF16)
        weight = lax.dot_general(spread, x_ref[:, model_width:], NT, preferred_element_type=F32)
        tile_copy(0, i).wait()
        tile_copy(1, i).wait()
        acts = lax.dot_general(
            buf[lax.rem(i, slots)], x_ref[:, :model_width], NT, preferred_element_type=F32
        )
        hidden = jax.nn.silu(acts[:step]) * acts[step:] * weight
        h_ref[:, pl.ds(pl.multiple_of(i * step, step), step)] = hidden.T.astype(BF16)

        @pl.when(i + slots < steps)
        def _():
            tile_copy(0, i + slots).start()
            tile_copy(1, i + slots).start()

        @pl.when(i + slots >= steps)
        def _():
            for k in range(per_step):
                j = (i + slots - steps) * per_step + k

                @pl.when(j < down_slots)
                def _():
                    down_copy(j).start()

        return carry

    lax.fori_loop(0, steps, hidden_step, 0)

    def down_step(j, carry):
        down_copy(j).wait()
        y_ref[:, pl.ds(pl.multiple_of(j * piece, piece), piece)] = jnp.dot(
            h_ref[...], down_buf[lax.rem(j, down_slots)], preferred_element_type=F32
        ).astype(BF16)

        @pl.when(j + down_slots < pieces)
        def _():
            down_copy(j + down_slots).start()

        return carry

    lax.fori_loop(0, pieces, down_step, 0)


def experts(rows, gate, up, down, first, width, expert_total):
    token_count = rows.shape[0]
    units, model_width = gate.shape
    step, piece = 2 * width, 512
    slots, down_slots = min(3, units // step), min(6, model_width // piece)
    whole = pl.BlockSpec(memory_space=pltpu.VMEM)
    away = pl.BlockSpec(memory_space=pl.ANY)
    return pl.pallas_call(
        functools.partial(experts_kernel, width, expert_total, step, piece, slots, down_slots),
        in_specs=[pl.BlockSpec(memory_space=pltpu.SMEM), whole, away, away, away],
        out_specs=whole,
        out_shape=jax.ShapeDtypeStruct((token_count, model_width), BF16),
        scratch_shapes=[
            pltpu.VMEM((token_count, units), BF16),
            pltpu.VMEM((slots, 2 * step, model_width), BF16),
            pltpu.VMEM((down_slots, units, piece), BF16),
            pltpu.SemaphoreType.DMA((2, slots)),
            pltpu.SemaphoreType.DMA((down_slots,)),
        ],
        compiler_params=pltpu.CompilerParams(vmem_limit_bytes=44 << 20),
        name="experts",
    )(first, rows, gate, up, down)


def experts_plain(rows, gate, up, down, first, width, expert_total):
    units, model_width = gate.shape
    x = rows[:, :model_width]
    gate_acts = lax.dot_general(x, gate, NT, preferred_element_type=F32)
    up_acts = lax.dot_general(x, up, NT, preferred_element_type=F32)
    row = jnp.arange(rows.shape[1] - model_width, dtype=jnp.int32)[:, None]
    expert = first[0] + jnp.arange(units, dtype=jnp.int32)[None, :] // width
    spread = (row % expert_total == expert).astype(BF16)
    weight = jnp.dot(rows[:, model_width:], spread, preferred_element_type=F32)
    hidden = (jax.nn.silu(gate_acts) * up_acts * weight).astype(BF16)
    return jnp.dot(hidden, down, preferred_element_type=F32).astype(BF16)


def local(tokens, expert_ids, gate_scores, gate_weight, up_weight, down_weight):
    model_width = tokens.shape[1]
    ep_count = lax.axis_size("ep")
    dp_count = lax.axis_size("dp")
    local_experts, _, width = gate_weight.shape
    expert_total = local_experts * ep_count
    gate = jnp.swapaxes(gate_weight, 1, 2).reshape(local_experts * width, model_width)
    up = jnp.swapaxes(up_weight, 1, 2).reshape(local_experts * width, model_width)
    down = down_weight.reshape(local_experts * width, model_width)
    first = (lax.axis_index("ep") * local_experts).astype(jnp.int32).reshape(1)

    sent = message(tokens, expert_ids, gate_scores, expert_total)

    powers = all(n & (n - 1) == 0 for n in (ep_count, dp_count))
    if powers and 2 <= ep_count <= 8 and 2 <= dp_count <= 8 and local_experts % 2 == 0:
        rows = gather_rows(sent, ep_count, dp_count)
        partial = experts(rows, gate, up, down, first, width, expert_total)
        return scatter_rows(partial, ep_count, dp_count)
    rows = lax.all_gather(sent, ("ep", "dp"), axis=0, tiled=True)
    partial = experts_plain(rows, gate, up, down, first, width, expert_total)
    return lax.psum_scatter(partial, ("ep", "dp"), scatter_dimension=0, tiled=True)


def solution(mesh):
    in_specs = (
        P(("rep", "ep", "dp"), None),
        P(("rep", "ep", "dp"), None),
        P(("rep", "ep", "dp"), None),
        P("ep", None, "dp"),
        P("ep", None, "dp"),
        P("ep", "dp", None),
    )
    out_specs = P(("rep", "ep", "dp"), None)
    return jax.shard_map(local, mesh=mesh, in_specs=in_specs, out_specs=out_specs, check_vma=False)
```

```python
import functools

import jax
import jax.numpy as jnp
from jax import lax
from jax.experimental import pallas as pl
from jax.experimental.pallas import tpu as pltpu
from jax.sharding import PartitionSpec as P

BF16 = jnp.bfloat16
F32 = jnp.float32
NT = (((1,), (1,)), ((), ()))


def add_up(*parts):
    total = parts[0].astype(F32)
    for part in parts[1:]:
        total = total + part.astype(F32)
    return total.astype(BF16)


def hop(x, ep_count, dp_count, ep_mask, dp_mask):
    pairs = [
        (i, ((i // dp_count) ^ ep_mask) * dp_count + ((i % dp_count) ^ dp_mask))
        for i in range(ep_count * dp_count)
    ]
    return lax.ppermute(x, ("ep", "dp"), pairs)


def ep_order(ep_count):
    return sorted(range(1, ep_count), key=lambda m: (-m.bit_length(), m))


def pack_kernel(*refs):
    out_ref = refs[-1]
    rows = refs[0].shape[0]
    for i, ref in enumerate(refs[:-1]):
        out_ref[i * rows : (i + 1) * rows, :] = ref[...]


def pack(blocks):
    whole = pl.BlockSpec(memory_space=pltpu.VMEM)
    shape = (len(blocks) * blocks[0].shape[0], blocks[0].shape[1])
    return pl.pallas_call(
        pack_kernel,
        in_specs=[whole] * len(blocks),
        out_specs=whole,
        out_shape=jax.ShapeDtypeStruct(shape, BF16),
        compiler_params=pltpu.CompilerParams(vmem_limit_bytes=3 << 20),
        name="pack",
    )(*blocks)


def gather_rows(x, ep_count, dp_count, fetches):
    send = functools.partial(hop, ep_count=ep_count, dp_count=dp_count)
    order = ep_order(ep_count)
    blocks = {(0, 0): x}
    for m in order:
        blocks[m, 0] = send(x, ep_mask=m, dp_mask=0)
    tiles = []
    if len(order) > 1:
        tile = fetches[0]([blocks[order[0], 0]])
        blocks[order[1], 0], tile = lax.optimization_barrier((blocks[order[1], 0], tile))
        tiles.append(tile)
    for d in range(2, dp_count, 2):
        for m in [0] + order:
            blocks[m, d] = send(blocks[m, 0], ep_mask=0, dp_mask=d)
    if dp_count > 2:
        last = order[-1]
        tile = fetches[len(tiles)]([blocks[last, 0]])
        blocks[last, 2], tile = lax.optimization_barrier((blocks[last, 2], tile))
        tiles.append(tile)
    near = pack([blocks[m, d] for d in range(0, dp_count, 2) for m in range(ep_count)])
    return near, send(near, ep_mask=0, dp_mask=1), tiles


def scatter_rows(y, ep_count, dp_count):
    send = functools.partial(hop, ep_count=ep_count, dp_count=dp_count)
    rows = y.shape[0]
    y = y.reshape(2, dp_count // 2, ep_count, rows // (ep_count * dp_count), y.shape[1])
    y = add_up(y[0], send(y[1], ep_mask=0, dp_mask=1))
    y = add_up(y[0], *[send(y[d // 2], ep_mask=0, dp_mask=d) for d in range(2, dp_count, 2)])
    return add_up(y[0], *[send(y[m], ep_mask=m, dp_mask=0) for m in ep_order(ep_count)])


def message_kernel(expert_total, tokens_ref, ids_ref, scores_ref, out_ref, ids_buf, scores_buf, sem):
    model_width = tokens_ref.shape[1]
    copies = [
        pltpu.make_async_copy(ids_ref, ids_buf, sem.at[0]),
        pltpu.make_async_copy(scores_ref, scores_buf, sem.at[1]),
        pltpu.make_async_copy(tokens_ref, out_ref.at[:, pl.ds(0, model_width)], sem.at[2]),
    ]
    for copy in copies:
        copy.start()
    copies[0].wait()
    copies[1].wait()
    weights = scores_buf[...] / jnp.sum(scores_buf[...], axis=1, keepdims=True)
    shape = (tokens_ref.shape[0], 2 * expert_total)
    column = lax.broadcasted_iota(jnp.int32, shape, 1)
    dense = jnp.zeros(shape, F32)
    for k in range(ids_ref.shape[1]):
        named = ids_buf[:, k : k + 1] == lax.rem(column, expert_total)
        dense = dense + jnp.where(named, weights[:, k : k + 1], 0.0)
    high = dense.astype(BF16).astype(F32)
    out_ref[:, model_width:] = jnp.where(column < expert_total, high, dense - high).astype(BF16)
    copies[2].wait()


def message(tokens, expert_ids, gate_scores, expert_total):
    shape = (tokens.shape[0], tokens.shape[1] + 2 * expert_total)
    operands = (tokens, expert_ids, gate_scores)
    return pl.pallas_call(
        functools.partial(message_kernel, expert_total),
        in_specs=[pl.BlockSpec(memory_space=pltpu.HBM)] * 3,
        out_specs=pl.BlockSpec(memory_space=pltpu.VMEM),
        out_shape=jax.ShapeDtypeStruct(shape, BF16),
        scratch_shapes=[
            pltpu.VMEM(expert_ids.shape, jnp.int32),
            pltpu.VMEM(gate_scores.shape, F32),
            pltpu.SemaphoreType.DMA((3,)),
        ],
        compiler_params=pltpu.CompilerParams(vmem_limit_bytes=4 << 20),
        name="message",
    )(*[pltpu.with_memory_space_constraint(a, pltpu.HBM) for a in operands])


def fetch_kernel(first_row, gate_ref, up_ref, *refs):
    out_ref, sem = refs[-2:]
    step = out_ref.shape[0] // 2
    copies = [
        pltpu.make_async_copy(
            ref.at[pl.ds(first_row, step), :], out_ref.at[pl.ds(k * step, step), :], sem.at[k]
        )
        for k, ref in enumerate((gate_ref, up_ref))
    ]
    for copy in copies:
        copy.start()
    for copy in copies:
        copy.wait()


def fetch(gate, up, tile, step, after):
    model_width = gate.shape[1]
    away = pl.BlockSpec(memory_space=pl.ANY)
    return pl.pallas_call(
        functools.partial(fetch_kernel, tile * step),
        in_specs=[away] * (2 + len(after)),
        out_specs=pl.BlockSpec(memory_space=pltpu.VMEM),
        out_shape=pltpu.VMEM((2 * step, model_width), BF16),
        scratch_shapes=[pltpu.SemaphoreType.DMA((2,))],
        compiler_params=pltpu.CompilerParams(vmem_limit_bytes=1 << 20),
        cost_estimate=pl.CostEstimate(
            flops=0, bytes_accessed=4 * step * model_width, transcendentals=0
        ),
        name="fetch",
    )(*[pltpu.with_memory_space_constraint(a, pltpu.HBM) for a in (gate, up)], *after)


def experts_kernel(width, expert_total, step, piece, slots, down_slots, held,
                   near_ref, far_ref, gate_ref, up_ref, down_ref, *refs):
    held_refs = refs[:held]
    y_ref, x_ref, h_ref, buf, down_buf, sem, down_sem = refs[held:]
    units, model_width = gate_ref.shape
    steps, pieces = units // step, model_width // piece
    per_step = -(-down_slots // slots)

    def tile_copy(which, i):
        slot = lax.rem(i, slots)
        return pltpu.make_async_copy(
            (gate_ref, up_ref)[which].at[pl.ds(pl.multiple_of(i * step, step), step), :],
            buf.at[slot, pl.ds(which * step, step), :],
            sem.at[which, slot],
        )

    def down_copy(j):
        slot = lax.rem(j, down_slots)
        return pltpu.make_async_copy(
            down_ref.at[:, pl.ds(pl.multiple_of(j * piece, piece), piece)],
            down_buf.at[slot],
            down_sem.at[slot],
        )

    for i in range(held, held + slots):
        tile_copy(0, i).start()
        tile_copy(1, i).start()

    first = lax.axis_index("ep") * (units // width)
    near_count = near_ref.shape[0]
    x_ref[:near_count, :] = near_ref[...]
    x_ref[near_count:, :] = far_ref[...]

    def hidden_tile(i, tile):
        shape = (step, x_ref.shape[1] - model_width)
        expert = first + (lax.broadcasted_iota(jnp.int32, shape, 0) + i * step) // width
        column = lax.rem(lax.broadcasted_iota(jnp.int32, shape, 1), expert_total)
        spread = (column == expert).astype(F32).astype(BF16)
        weight = lax.dot_general(spread, x_ref[:, model_width:], NT, preferred_element_type=F32)
        acts = lax.dot_general(tile[...], x_ref[:, :model_width], NT, preferred_element_type=F32)
        hidden = jax.nn.silu(acts[:step]) * acts[step:] * weight
        h_ref[:, pl.ds(pl.multiple_of(i * step, step), step)] = hidden.T.astype(BF16)

    def hidden_step(i, carry):
        tile_copy(0, i).wait()
        tile_copy(1, i).wait()
        hidden_tile(i, buf.at[lax.rem(i, slots)])

        @pl.when(i + slots < steps)
        def _():
            tile_copy(0, i + slots).start()
            tile_copy(1, i + slots).start()

        @pl.when(i + slots >= steps)
        def _():
            for k in range(per_step):
                j = (i + slots - steps) * per_step + k

                @pl.when(j < down_slots)
                def _():
                    down_copy(j).start()

        return carry

    for i in range(held):
        hidden_tile(i, held_refs[i])
    lax.fori_loop(held, steps, hidden_step, 0)

    def down_step(j, carry):
        down_copy(j).wait()
        y_ref[:, pl.ds(pl.multiple_of(j * piece, piece), piece)] = jnp.dot(
            h_ref[...], down_buf[lax.rem(j, down_slots)], preferred_element_type=F32
        ).astype(BF16)

        @pl.when(j + down_slots < pieces)
        def _():
            down_copy(j + down_slots).start()

        return carry

    lax.fori_loop(0, pieces, down_step, 0)


def experts(near, far, gate, up, down, width, expert_total, tiles):
    token_count = near.shape[0] + far.shape[0]
    units, model_width = gate.shape
    step, piece = 2 * width, 512
    slots, down_slots = min(2, units // step - len(tiles)), min(5, model_width // piece)
    whole = pl.BlockSpec(memory_space=pltpu.VMEM)
    away = pl.BlockSpec(memory_space=pl.ANY)
    return pl.pallas_call(
        functools.partial(
            experts_kernel, width, expert_total, step, piece, slots, down_slots, len(tiles)
        ),
        in_specs=[whole, whole, away, away, away]
        + [whole] * len(tiles),
        out_specs=whole,
        out_shape=jax.ShapeDtypeStruct((token_count, model_width), BF16),
        scratch_shapes=[
            pltpu.VMEM((token_count, near.shape[1]), BF16),
            pltpu.VMEM((token_count, units), BF16),
            pltpu.VMEM((slots, 2 * step, model_width), BF16),
            pltpu.VMEM((down_slots, units, piece), BF16),
            pltpu.SemaphoreType.DMA((2, slots)),
            pltpu.SemaphoreType.DMA((down_slots,)),
        ],
        compiler_params=pltpu.CompilerParams(vmem_limit_bytes=34 << 20),
        name="experts",
    )(
        near,
        far,
        *[pltpu.with_memory_space_constraint(a, pltpu.HBM) for a in (gate, up, down)],
        *[pltpu.with_memory_space_constraint(t, pltpu.VMEM) for t in tiles],
    )


def experts_plain(rows, gate, up, down, first, width, expert_total):
    units, model_width = gate.shape
    x = rows[:, :model_width]
    gate_acts = lax.dot_general(x, gate, NT, preferred_element_type=F32)
    up_acts = lax.dot_general(x, up, NT, preferred_element_type=F32)
    row = jnp.arange(rows.shape[1] - model_width, dtype=jnp.int32)[:, None]
    expert = first[0] + jnp.arange(units, dtype=jnp.int32)[None, :] // width
    spread = (row % expert_total == expert).astype(BF16)
    weight = jnp.dot(rows[:, model_width:], spread, preferred_element_type=F32)
    hidden = (jax.nn.silu(gate_acts) * up_acts * weight).astype(BF16)
    return jnp.dot(hidden, down, preferred_element_type=F32).astype(BF16)


def local(tokens, expert_ids, gate_scores, gate_weight, up_weight, down_weight):
    model_width = tokens.shape[1]
    ep_count = lax.axis_size("ep")
    dp_count = lax.axis_size("dp")
    local_experts, _, width = gate_weight.shape
    expert_total = local_experts * ep_count
    gate = jnp.swapaxes(gate_weight, 1, 2).reshape(local_experts * width, model_width)
    up = jnp.swapaxes(up_weight, 1, 2).reshape(local_experts * width, model_width)
    down = down_weight.reshape(local_experts * width, model_width)
    first = (lax.axis_index("ep") * local_experts).astype(jnp.int32).reshape(1)

    sent = message(tokens, expert_ids, gate_scores, expert_total)

    powers = all(n & (n - 1) == 0 for n in (ep_count, dp_count))
    if powers and 2 <= ep_count <= 8 and 2 <= dp_count <= 8 and local_experts % 2 == 0 and local_experts >= 8:
        fetches = [functools.partial(fetch, gate, up, tile, 2 * width) for tile in range(2)]
        near, far, tiles = gather_rows(sent, ep_count, dp_count, fetches)
        partial = experts(near, far, gate, up, down, width, expert_total, tiles)
        return scatter_rows(partial, ep_count, dp_count)
    rows = lax.all_gather(sent, ("ep", "dp"), axis=0, tiled=True)
    partial = experts_plain(rows, gate, up, down, first, width, expert_total)
    return lax.psum_scatter(partial, ("ep", "dp"), scatter_dimension=0, tiled=True)


def solution(mesh):
    in_specs = (
        P(("rep", "ep", "dp"), None),
        P(("rep", "ep", "dp"), None),
        P(("rep", "ep", "dp"), None),
        P("ep", None, "dp"),
        P("ep", None, "dp"),
        P("ep", "dp", None),
    )
    out_specs = P(("rep", "ep", "dp"), None)
    return jax.shard_map(local, mesh=mesh, in_specs=in_specs, out_specs=out_specs, check_vma=False)
```

```python
import functools

import jax
import jax.numpy as jnp
from jax import lax
from jax.experimental import pallas as pl
from jax.experimental.pallas import tpu as pltpu
from jax.sharding import PartitionSpec as P

BF16 = jnp.bfloat16
F32 = jnp.float32
NT = (((1,), (1,)), ((), ()))


def add_up(*parts):
    total = parts[0].astype(F32)
    for part in parts[1:]:
        total = total + part.astype(F32)
    return total.astype(BF16)


def hop(x, ep_count, dp_count, ep_mask, dp_mask):
    pairs = [
        (i, ((i // dp_count) ^ ep_mask) * dp_count + ((i % dp_count) ^ dp_mask))
        for i in range(ep_count * dp_count)
    ]
    return lax.ppermute(x, ("ep", "dp"), pairs)


def ep_order(ep_count):
    return sorted(range(1, ep_count), key=lambda m: (-m.bit_length(), m))


def gather_rows(x, ep_count, dp_count):
    send = functools.partial(hop, ep_count=ep_count, dp_count=dp_count)
    blocks = {(0, 0): x}
    for m in ep_order(ep_count):
        blocks[m, 0] = send(x, ep_mask=m, dp_mask=0)
    for d in range(2, dp_count, 2):
        for m in [0] + ep_order(ep_count):
            blocks[m, d] = send(blocks[m, 0], ep_mask=0, dp_mask=d)
    near = jnp.concatenate(
        [blocks[m, d] for d in range(0, dp_count, 2) for m in range(ep_count)], axis=0
    )
    return jnp.concatenate([near, send(near, ep_mask=0, dp_mask=1)], axis=0)


def scatter_rows(y, ep_count, dp_count):
    send = functools.partial(hop, ep_count=ep_count, dp_count=dp_count)
    rows = y.shape[0]
    y = y.reshape(2, dp_count // 2, ep_count, rows // (ep_count * dp_count), y.shape[1])
    y = add_up(y[0], send(y[1], ep_mask=0, dp_mask=1))
    y = add_up(y[0], *[send(y[d // 2], ep_mask=0, dp_mask=d) for d in range(2, dp_count, 2)])
    return add_up(y[0], *[send(y[m], ep_mask=m, dp_mask=0) for m in ep_order(ep_count)])


def message_kernel(expert_total, tokens_ref, ids_ref, scores_ref, out_ref, ids_buf, scores_buf, sem):
    model_width = tokens_ref.shape[1]
    copies = [
        pltpu.make_async_copy(ids_ref, ids_buf, sem.at[0]),
        pltpu.make_async_copy(scores_ref, scores_buf, sem.at[1]),
        pltpu.make_async_copy(tokens_ref, out_ref.at[:, pl.ds(0, model_width)], sem.at[2]),
    ]
    for copy in copies:
        copy.start()
    copies[0].wait()
    copies[1].wait()
    weights = scores_buf[...] / jnp.sum(scores_buf[...], axis=1, keepdims=True)
    shape = (tokens_ref.shape[0], 2 * expert_total)
    column = lax.broadcasted_iota(jnp.int32, shape, 1)
    dense = jnp.zeros(shape, F32)
    for k in range(ids_ref.shape[1]):
        named = ids_buf[:, k : k + 1] == lax.rem(column, expert_total)
        dense = dense + jnp.where(named, weights[:, k : k + 1], 0.0)
    high = dense.astype(BF16).astype(F32)
    out_ref[:, model_width:] = jnp.where(column < expert_total, high, dense - high).astype(BF16)
    copies[2].wait()


def message(tokens, expert_ids, gate_scores, expert_total):
    shape = (tokens.shape[0], tokens.shape[1] + 2 * expert_total)
    operands = (tokens, expert_ids, gate_scores)
    return pl.pallas_call(
        functools.partial(message_kernel, expert_total),
        in_specs=[pl.BlockSpec(memory_space=pltpu.HBM)] * 3,
        out_specs=pl.BlockSpec(memory_space=pltpu.VMEM),
        out_shape=jax.ShapeDtypeStruct(shape, BF16),
        scratch_shapes=[
            pltpu.VMEM(expert_ids.shape, jnp.int32),
            pltpu.VMEM(gate_scores.shape, F32),
            pltpu.SemaphoreType.DMA((3,)),
        ],
        compiler_params=pltpu.CompilerParams(vmem_limit_bytes=4 << 20),
        name="message",
    )(*[pltpu.with_memory_space_constraint(a, pltpu.HBM) for a in operands])


def experts_kernel(width, expert_total, step, piece, slots, down_slots,
                   first_ref, x_ref, gate_ref, up_ref, down_ref, y_ref,
                   h_ref, buf, down_buf, sem, down_sem):
    units, model_width = gate_ref.shape
    steps, pieces = units // step, model_width // piece
    per_step = -(-down_slots // slots)

    def tile_copy(which, i):
        slot = lax.rem(i, slots)
        return pltpu.make_async_copy(
            (gate_ref, up_ref)[which].at[pl.ds(pl.multiple_of(i * step, step), step), :],
            buf.at[slot, pl.ds(which * step, step), :],
            sem.at[which, slot],
        )

    def down_copy(j):
        slot = lax.rem(j, down_slots)
        return pltpu.make_async_copy(
            down_ref.at[:, pl.ds(pl.multiple_of(j * piece, piece), piece)],
            down_buf.at[slot],
            down_sem.at[slot],
        )

    for i in range(slots):
        tile_copy(0, i).start()
        tile_copy(1, i).start()

    def hidden_step(i, carry):
        shape = (step, x_ref.shape[1] - model_width)
        expert = first_ref[0] + (lax.broadcasted_iota(jnp.int32, shape, 0) + i * step) // width
        column = lax.rem(lax.broadcasted_iota(jnp.int32, shape, 1), expert_total)
        spread = (column == expert).astype(F32).astype(BF16)
        weight = lax.dot_general(spread, x_ref[:, model_width:], NT, preferred_element_type=F32)
        tile_copy(0, i).wait()
        tile_copy(1, i).wait()
        acts = lax.dot_general(
            buf[lax.rem(i, slots)], x_ref[:, :model_width], NT, preferred_element_type=F32
        )
        hidden = jax.nn.silu(acts[:step]) * acts[step:] * weight
        h_ref[:, pl.ds(pl.multiple_of(i * step, step), step)] = hidden.T.astype(BF16)

        @pl.when(i + slots < steps)
        def _():
            tile_copy(0, i + slots).start()
            tile_copy(1, i + slots).start()

        @pl.when(i + slots >= steps)
        def _():
            for k in range(per_step):
                j = (i + slots - steps) * per_step + k

                @pl.when(j < down_slots)
                def _():
                    down_copy(j).start()

        return carry

    lax.fori_loop(0, steps, hidden_step, 0)

    def down_step(j, carry):
        down_copy(j).wait()
        y_ref[:, pl.ds(pl.multiple_of(j * piece, piece), piece)] = jnp.dot(
            h_ref[...], down_buf[lax.rem(j, down_slots)], preferred_element_type=F32
        ).astype(BF16)

        @pl.when(j + down_slots < pieces)
        def _():
            down_copy(j + down_slots).start()

        return carry

    lax.fori_loop(0, pieces, down_step, 0)


def experts(rows, gate, up, down, first, width, expert_total):
    token_count = rows.shape[0]
    units, model_width = gate.shape
    step, piece = 2 * width, 512
    slots, down_slots = min(3, units // step), min(6, model_width // piece)
    whole = pl.BlockSpec(memory_space=pltpu.VMEM)
    away = pl.BlockSpec(memory_space=pl.ANY)
    return pl.pallas_call(
        functools.partial(experts_kernel, width, expert_total, step, piece, slots, down_slots),
        in_specs=[pl.BlockSpec(memory_space=pltpu.SMEM), whole, away, away, away],
        out_specs=whole,
        out_shape=jax.ShapeDtypeStruct((token_count, model_width), BF16),
        scratch_shapes=[
            pltpu.VMEM((token_count, units), BF16),
            pltpu.VMEM((slots, 2 * step, model_width), BF16),
            pltpu.VMEM((down_slots, units, piece), BF16),
            pltpu.SemaphoreType.DMA((2, slots)),
            pltpu.SemaphoreType.DMA((down_slots,)),
        ],
        compiler_params=pltpu.CompilerParams(vmem_limit_bytes=44 << 20),
        name="experts",
    )(first, rows, gate, up, down)


def experts_plain(rows, gate, up, down, first, width, expert_total):
    units, model_width = gate.shape
    x = rows[:, :model_width]
    gate_acts = lax.dot_general(x, gate, NT, preferred_element_type=F32)
    up_acts = lax.dot_general(x, up, NT, preferred_element_type=F32)
    row = jnp.arange(rows.shape[1] - model_width, dtype=jnp.int32)[:, None]
    expert = first[0] + jnp.arange(units, dtype=jnp.int32)[None, :] // width
    spread = (row % expert_total == expert).astype(BF16)
    weight = jnp.dot(rows[:, model_width:], spread, preferred_element_type=F32)
    hidden = (jax.nn.silu(gate_acts) * up_acts * weight).astype(BF16)
    return jnp.dot(hidden, down, preferred_element_type=F32).astype(BF16)


def local(tokens, expert_ids, gate_scores, gate_weight, up_weight, down_weight):
    model_width = tokens.shape[1]
    ep_count = lax.axis_size("ep")
    dp_count = lax.axis_size("dp")
    local_experts, _, width = gate_weight.shape
    expert_total = local_experts * ep_count
    gate = jnp.swapaxes(gate_weight, 1, 2).reshape(local_experts * width, model_width)
    up = jnp.swapaxes(up_weight, 1, 2).reshape(local_experts * width, model_width)
    down = down_weight.reshape(local_experts * width, model_width)
    first = (lax.axis_index("ep") * local_experts).astype(jnp.int32).reshape(1)

    sent = message(tokens, expert_ids, gate_scores, expert_total)

    powers = all(n & (n - 1) == 0 for n in (ep_count, dp_count))
    if powers and 2 <= ep_count <= 8 and 2 <= dp_count <= 8 and local_experts % 2 == 0:
        rows = gather_rows(sent, ep_count, dp_count)
        partial = experts(rows, gate, up, down, first, width, expert_total)
        return scatter_rows(partial, ep_count, dp_count)
    rows = lax.all_gather(sent, ("ep", "dp"), axis=0, tiled=True)
    partial = experts_plain(rows, gate, up, down, first, width, expert_total)
    return lax.psum_scatter(partial, ("ep", "dp"), scatter_dimension=0, tiled=True)


def solution(mesh):
    in_specs = (
        P(("rep", "ep", "dp"), None),
        P(("rep", "ep", "dp"), None),
        P(("rep", "ep", "dp"), None),
        P("ep", None, "dp"),
        P("ep", None, "dp"),
        P("ep", "dp", None),
    )
    out_specs = P(("rep", "ep", "dp"), None)
    return jax.shard_map(local, mesh=mesh, in_specs=in_specs, out_specs=out_specs, check_vma=False)
```

```python
import functools

import jax
import jax.numpy as jnp
from jax import lax
from jax.experimental import pallas as pl
from jax.experimental.pallas import tpu as pltpu
from jax.sharding import PartitionSpec as P

BF16 = jnp.bfloat16
F32 = jnp.float32
NT = (((1,), (1,)), ((), ()))


def add_up(*parts):
    total = parts[0].astype(F32)
    for part in parts[1:]:
        total = total + part.astype(F32)
    return total.astype(BF16)


def hop(x, ep_count, dp_count, ep_mask, dp_mask):
    pairs = [
        (i, ((i // dp_count) ^ ep_mask) * dp_count + ((i % dp_count) ^ dp_mask))
        for i in range(ep_count * dp_count)
    ]
    return lax.ppermute(x, ("ep", "dp"), pairs)


def ep_order(ep_count):
    return sorted(range(1, ep_count), key=lambda m: (-m.bit_length(), m))


def gather_rows(x, ep_count, dp_count):
    send = functools.partial(hop, ep_count=ep_count, dp_count=dp_count)
    blocks = {(0, 0): x}
    for m in ep_order(ep_count):
        blocks[m, 0] = send(x, ep_mask=m, dp_mask=0)
    for d in range(2, dp_count, 2):
        for m in [0] + ep_order(ep_count):
            blocks[m, d] = send(blocks[m, 0], ep_mask=0, dp_mask=d)
    near = jnp.concatenate(
        [blocks[m, d] for d in range(0, dp_count, 2) for m in range(ep_count)], axis=0
    )
    return jnp.concatenate([near, send(near, ep_mask=0, dp_mask=1)], axis=0)


def scatter_rows(y, ep_count, dp_count):
    send = functools.partial(hop, ep_count=ep_count, dp_count=dp_count)
    rows = y.shape[0]
    y = y.reshape(2, dp_count // 2, ep_count, rows // (ep_count * dp_count), y.shape[1])
    y = add_up(y[0], send(y[1], ep_mask=0, dp_mask=1))
    order = ep_order(ep_count)
    far = []
    for d in range(2, dp_count, 2):
        block = y[d // 2]
        block = add_up(block[0], *[send(block[m], ep_mask=m, dp_mask=0) for m in order])
        far.append(send(block, ep_mask=0, dp_mask=d))
    return add_up(y[0, 0], *[send(y[0, m], ep_mask=m, dp_mask=0) for m in order], *far)


def message_kernel(expert_total, tokens_ref, ids_ref, scores_ref, out_ref, ids_buf, scores_buf, sem):
    model_width = tokens_ref.shape[1]
    copies = [
        pltpu.make_async_copy(ids_ref, ids_buf, sem.at[0]),
        pltpu.make_async_copy(scores_ref, scores_buf, sem.at[1]),
        pltpu.make_async_copy(tokens_ref, out_ref.at[:, pl.ds(0, model_width)], sem.at[2]),
    ]
    for copy in copies:
        copy.start()
    copies[0].wait()
    copies[1].wait()
    weights = scores_buf[...] / jnp.sum(scores_buf[...], axis=1, keepdims=True)
    shape = (tokens_ref.shape[0], 2 * expert_total)
    column = lax.broadcasted_iota(jnp.int32, shape, 1)
    dense = jnp.zeros(shape, F32)
    for k in range(ids_ref.shape[1]):
        named = ids_buf[:, k : k + 1] == lax.rem(column, expert_total)
        dense = dense + jnp.where(named, weights[:, k : k + 1], 0.0)
    high = dense.astype(BF16).astype(F32)
    out_ref[:, model_width:] = jnp.where(column < expert_total, high, dense - high).astype(BF16)
    copies[2].wait()


def message(tokens, expert_ids, gate_scores, expert_total):
    shape = (tokens.shape[0], tokens.shape[1] + 2 * expert_total)
    operands = (tokens, expert_ids, gate_scores)
    return pl.pallas_call(
        functools.partial(message_kernel, expert_total),
        in_specs=[pl.BlockSpec(memory_space=pltpu.HBM)] * 3,
        out_specs=pl.BlockSpec(memory_space=pltpu.VMEM),
        out_shape=jax.ShapeDtypeStruct(shape, BF16),
        scratch_shapes=[
            pltpu.VMEM(expert_ids.shape, jnp.int32),
            pltpu.VMEM(gate_scores.shape, F32),
            pltpu.SemaphoreType.DMA((3,)),
        ],
        compiler_params=pltpu.CompilerParams(vmem_limit_bytes=4 << 20),
        name="message",
    )(*[pltpu.with_memory_space_constraint(a, pltpu.HBM) for a in operands])


def experts_kernel(width, expert_total, step, piece, slots, down_slots,
                   first_ref, x_ref, gate_ref, up_ref, down_ref, y_ref,
                   h_ref, buf, down_buf, sem, down_sem):
    units, model_width = gate_ref.shape
    steps, pieces = units // step, model_width // piece
    per_step = -(-down_slots // slots)

    def tile_copy(which, i):
        slot = lax.rem(i, slots)
        return pltpu.make_async_copy(
            (gate_ref, up_ref)[which].at[pl.ds(pl.multiple_of(i * step, step), step), :],
            buf.at[slot, pl.ds(which * step, step), :],
            sem.at[which, slot],
        )

    def down_copy(j):
        slot = lax.rem(j, down_slots)
        return pltpu.make_async_copy(
            down_ref.at[:, pl.ds(pl.multiple_of(j * piece, piece), piece)],
            down_buf.at[slot],
            down_sem.at[slot],
        )

    for i in range(slots):
        tile_copy(0, i).start()
        tile_copy(1, i).start()

    def hidden_step(i, carry):
        shape = (step, x_ref.shape[1] - model_width)
        expert = first_ref[0] + (lax.broadcasted_iota(jnp.int32, shape, 0) + i * step) // width
        column = lax.rem(lax.broadcasted_iota(jnp.int32, shape, 1), expert_total)
        spread = (column == expert).astype(F32).astype(BF16)
        weight = lax.dot_general(spread, x_ref[:, model_width:], NT, preferred_element_type=F32)
        tile_copy(0, i).wait()
        tile_copy(1, i).wait()
        acts = lax.dot_general(
            buf[lax.rem(i, slots)], x_ref[:, :model_width], NT, preferred_element_type=F32
        )
        hidden = jax.nn.silu(acts[:step]) * acts[step:] * weight
        h_ref[:, pl.ds(pl.multiple_of(i * step, step), step)] = hidden.T.astype(BF16)

        @pl.when(i + slots < steps)
        def _():
            tile_copy(0, i + slots).start()
            tile_copy(1, i + slots).start()

        @pl.when(i + slots >= steps)
        def _():
            for k in range(per_step):
                j = (i + slots - steps) * per_step + k

                @pl.when(j < down_slots)
                def _():
                    down_copy(j).start()

        return carry

    lax.fori_loop(0, steps, hidden_step, 0)

    def down_step(j, carry):
        down_copy(j).wait()
        y_ref[:, pl.ds(pl.multiple_of(j * piece, piece), piece)] = jnp.dot(
            h_ref[...], down_buf[lax.rem(j, down_slots)], preferred_element_type=F32
        ).astype(BF16)

        @pl.when(j + down_slots < pieces)
        def _():
            down_copy(j + down_slots).start()

        return carry

    lax.fori_loop(0, pieces, down_step, 0)


def experts(rows, gate, up, down, first, width, expert_total):
    token_count = rows.shape[0]
    units, model_width = gate.shape
    step, piece = 2 * width, 512
    slots, down_slots = min(3, units // step), min(6, model_width // piece)
    whole = pl.BlockSpec(memory_space=pltpu.VMEM)
    away = pl.BlockSpec(memory_space=pl.ANY)
    return pl.pallas_call(
        functools.partial(experts_kernel, width, expert_total, step, piece, slots, down_slots),
        in_specs=[pl.BlockSpec(memory_space=pltpu.SMEM), whole, away, away, away],
        out_specs=whole,
        out_shape=jax.ShapeDtypeStruct((token_count, model_width), BF16),
        scratch_shapes=[
            pltpu.VMEM((token_count, units), BF16),
            pltpu.VMEM((slots, 2 * step, model_width), BF16),
            pltpu.VMEM((down_slots, units, piece), BF16),
            pltpu.SemaphoreType.DMA((2, slots)),
            pltpu.SemaphoreType.DMA((down_slots,)),
        ],
        compiler_params=pltpu.CompilerParams(vmem_limit_bytes=44 << 20),
        name="experts",
    )(first, rows, gate, up, down)


def experts_plain(rows, gate, up, down, first, width, expert_total):
    units, model_width = gate.shape
    x = rows[:, :model_width]
    gate_acts = lax.dot_general(x, gate, NT, preferred_element_type=F32)
    up_acts = lax.dot_general(x, up, NT, preferred_element_type=F32)
    row = jnp.arange(rows.shape[1] - model_width, dtype=jnp.int32)[:, None]
    expert = first[0] + jnp.arange(units, dtype=jnp.int32)[None, :] // width
    spread = (row % expert_total == expert).astype(BF16)
    weight = jnp.dot(rows[:, model_width:], spread, preferred_element_type=F32)
    hidden = (jax.nn.silu(gate_acts) * up_acts * weight).astype(BF16)
    return jnp.dot(hidden, down, preferred_element_type=F32).astype(BF16)


def local(tokens, expert_ids, gate_scores, gate_weight, up_weight, down_weight):
    model_width = tokens.shape[1]
    ep_count = lax.axis_size("ep")
    dp_count = lax.axis_size("dp")
    local_experts, _, width = gate_weight.shape
    expert_total = local_experts * ep_count
    gate = jnp.swapaxes(gate_weight, 1, 2).reshape(local_experts * width, model_width)
    up = jnp.swapaxes(up_weight, 1, 2).reshape(local_experts * width, model_width)
    down = down_weight.reshape(local_experts * width, model_width)
    first = (lax.axis_index("ep") * local_experts).astype(jnp.int32).reshape(1)

    sent = message(tokens, expert_ids, gate_scores, expert_total)

    powers = all(n & (n - 1) == 0 for n in (ep_count, dp_count))
    if powers and 2 <= ep_count <= 8 and 2 <= dp_count <= 8 and local_experts % 2 == 0:
        rows = gather_rows(sent, ep_count, dp_count)
        partial = experts(rows, gate, up, down, first, width, expert_total)
        return scatter_rows(partial, ep_count, dp_count)
    rows = lax.all_gather(sent, ("ep", "dp"), axis=0, tiled=True)
    partial = experts_plain(rows, gate, up, down, first, width, expert_total)
    return lax.psum_scatter(partial, ("ep", "dp"), scatter_dimension=0, tiled=True)


def solution(mesh):
    in_specs = (
        P(("rep", "ep", "dp"), None),
        P(("rep", "ep", "dp"), None),
        P(("rep", "ep", "dp"), None),
        P("ep", None, "dp"),
        P("ep", None, "dp"),
        P("ep", "dp", None),
    )
    out_specs = P(("rep", "ep", "dp"), None)
    return jax.shard_map(local, mesh=mesh, in_specs=in_specs, out_specs=out_specs, check_vma=False)
```

```python
import functools

import jax
import jax.numpy as jnp
from jax import lax
from jax.experimental import pallas as pl
from jax.experimental.pallas import tpu as pltpu
from jax.sharding import PartitionSpec as P

BF16 = jnp.bfloat16
F32 = jnp.float32
NT = (((1,), (1,)), ((), ()))


def add_up(*parts):
    total = parts[0].astype(F32)
    for part in parts[1:]:
        total = total + part.astype(F32)
    return total.astype(BF16)


def hop(x, ep_count, dp_count, ep_mask, dp_mask):
    pairs = [
        (i, ((i // dp_count) ^ ep_mask) * dp_count + ((i % dp_count) ^ dp_mask))
        for i in range(ep_count * dp_count)
    ]
    return lax.ppermute(x, ("ep", "dp"), pairs)


def ep_order(ep_count):
    return sorted(range(1, ep_count), key=lambda m: (-m.bit_length(), m))


def gather_rows(x, ep_count, dp_count):
    send = functools.partial(hop, ep_count=ep_count, dp_count=dp_count)
    blocks = {(0, 0): x}
    for m in ep_order(ep_count):
        blocks[m, 0] = send(x, ep_mask=m, dp_mask=0)
    for d in range(2, dp_count, 2):
        for m in [0] + ep_order(ep_count):
            blocks[m, d] = send(blocks[m, 0], ep_mask=0, dp_mask=d)
    near = jnp.concatenate(
        [blocks[m, d] for d in range(0, dp_count, 2) for m in range(ep_count)], axis=0
    )
    return jnp.concatenate([near, send(near, ep_mask=0, dp_mask=1)], axis=0)


def scatter_rows(y, ep_count, dp_count):
    send = functools.partial(hop, ep_count=ep_count, dp_count=dp_count)
    rows = y.shape[0]
    y = y.reshape(2, dp_count // 2, ep_count, rows // (ep_count * dp_count), y.shape[1])
    y = add_up(y[0], send(y[1], ep_mask=0, dp_mask=1))
    order = list(range(ep_count - 1, 0, -1))
    far = []
    for d in range(2, dp_count, 2):
        block = y[d // 2]
        block = add_up(block[0], *[send(block[m], ep_mask=m, dp_mask=0) for m in order])
        far.append(send(block, ep_mask=0, dp_mask=d))
    return add_up(y[0, 0], *[send(y[0, m], ep_mask=m, dp_mask=0) for m in order], *far)


def message_kernel(expert_total, tokens_ref, ids_ref, scores_ref, out_ref, ids_buf, scores_buf, sem):
    model_width = tokens_ref.shape[1]
    copies = [
        pltpu.make_async_copy(ids_ref, ids_buf, sem.at[0]),
        pltpu.make_async_copy(scores_ref, scores_buf, sem.at[1]),
        pltpu.make_async_copy(tokens_ref, out_ref.at[:, pl.ds(0, model_width)], sem.at[2]),
    ]
    for copy in copies:
        copy.start()
    copies[0].wait()
    copies[1].wait()
    weights = scores_buf[...] / jnp.sum(scores_buf[...], axis=1, keepdims=True)
    shape = (tokens_ref.shape[0], 2 * expert_total)
    column = lax.broadcasted_iota(jnp.int32, shape, 1)
    dense = jnp.zeros(shape, F32)
    for k in range(ids_ref.shape[1]):
        named = ids_buf[:, k : k + 1] == lax.rem(column, expert_total)
        dense = dense + jnp.where(named, weights[:, k : k + 1], 0.0)
    high = dense.astype(BF16).astype(F32)
    out_ref[:, model_width:] = jnp.where(column < expert_total, high, dense - high).astype(BF16)
    copies[2].wait()


def message(tokens, expert_ids, gate_scores, expert_total):
    shape = (tokens.shape[0], tokens.shape[1] + 2 * expert_total)
    operands = (tokens, expert_ids, gate_scores)
    return pl.pallas_call(
        functools.partial(message_kernel, expert_total),
        in_specs=[pl.BlockSpec(memory_space=pltpu.HBM)] * 3,
        out_specs=pl.BlockSpec(memory_space=pltpu.VMEM),
        out_shape=jax.ShapeDtypeStruct(shape, BF16),
        scratch_shapes=[
            pltpu.VMEM(expert_ids.shape, jnp.int32),
            pltpu.VMEM(gate_scores.shape, F32),
            pltpu.SemaphoreType.DMA((3,)),
        ],
        compiler_params=pltpu.CompilerParams(vmem_limit_bytes=4 << 20),
        name="message",
    )(*[pltpu.with_memory_space_constraint(a, pltpu.HBM) for a in operands])


def experts_kernel(width, expert_total, step, piece, slots, down_slots,
                   first_ref, x_ref, gate_ref, up_ref, down_ref, y_ref,
                   h_ref, buf, down_buf, sem, down_sem):
    units, model_width = gate_ref.shape
    steps, pieces = units // step, model_width // piece
    per_step = -(-down_slots // slots)

    def tile_copy(which, i):
        slot = lax.rem(i, slots)
        return pltpu.make_async_copy(
            (gate_ref, up_ref)[which].at[pl.ds(pl.multiple_of(i * step, step), step), :],
            buf.at[slot, pl.ds(which * step, step), :],
            sem.at[which, slot],
        )

    def down_copy(j):
        slot = lax.rem(j, down_slots)
        return pltpu.make_async_copy(
            down_ref.at[:, pl.ds(pl.multiple_of(j * piece, piece), piece)],
            down_buf.at[slot],
            down_sem.at[slot],
        )

    for i in range(slots):
        tile_copy(0, i).start()
        tile_copy(1, i).start()

    def hidden_step(i, carry):
        shape = (step, x_ref.shape[1] - model_width)
        expert = first_ref[0] + (lax.broadcasted_iota(jnp.int32, shape, 0) + i * step) // width
        column = lax.rem(lax.broadcasted_iota(jnp.int32, shape, 1), expert_total)
        spread = (column == expert).astype(F32).astype(BF16)
        weight = lax.dot_general(spread, x_ref[:, model_width:], NT, preferred_element_type=F32)
        tile_copy(0, i).wait()
        tile_copy(1, i).wait()
        acts = lax.dot_general(
            buf[lax.rem(i, slots)], x_ref[:, :model_width], NT, preferred_element_type=F32
        )
        hidden = jax.nn.silu(acts[:step]) * acts[step:] * weight
        h_ref[:, pl.ds(pl.multiple_of(i * step, step), step)] = hidden.T.astype(BF16)

        @pl.when(i + slots < steps)
        def _():
            tile_copy(0, i + slots).start()
            tile_copy(1, i + slots).start()

        @pl.when(i + slots >= steps)
        def _():
            for k in range(per_step):
                j = (i + slots - steps) * per_step + k

                @pl.when(j < down_slots)
                def _():
                    down_copy(j).start()

        return carry

    lax.fori_loop(0, steps, hidden_step, 0)

    def down_step(j, carry):
        down_copy(j).wait()
        y_ref[:, pl.ds(pl.multiple_of(j * piece, piece), piece)] = jnp.dot(
            h_ref[...], down_buf[lax.rem(j, down_slots)], preferred_element_type=F32
        ).astype(BF16)

        @pl.when(j + down_slots < pieces)
        def _():
            down_copy(j + down_slots).start()

        return carry

    lax.fori_loop(0, pieces, down_step, 0)


def experts(rows, gate, up, down, first, width, expert_total):
    token_count = rows.shape[0]
    units, model_width = gate.shape
    step, piece = 2 * width, 512
    slots, down_slots = min(3, units // step), min(6, model_width // piece)
    whole = pl.BlockSpec(memory_space=pltpu.VMEM)
    away = pl.BlockSpec(memory_space=pl.ANY)
    return pl.pallas_call(
        functools.partial(experts_kernel, width, expert_total, step, piece, slots, down_slots),
        in_specs=[pl.BlockSpec(memory_space=pltpu.SMEM), whole, away, away, away],
        out_specs=whole,
        out_shape=jax.ShapeDtypeStruct((token_count, model_width), BF16),
        scratch_shapes=[
            pltpu.VMEM((token_count, units), BF16),
            pltpu.VMEM((slots, 2 * step, model_width), BF16),
            pltpu.VMEM((down_slots, units, piece), BF16),
            pltpu.SemaphoreType.DMA((2, slots)),
            pltpu.SemaphoreType.DMA((down_slots,)),
        ],
        compiler_params=pltpu.CompilerParams(vmem_limit_bytes=44 << 20),
        name="experts",
    )(first, rows, gate, up, down)


def experts_plain(rows, gate, up, down, first, width, expert_total):
    units, model_width = gate.shape
    x = rows[:, :model_width]
    gate_acts = lax.dot_general(x, gate, NT, preferred_element_type=F32)
    up_acts = lax.dot_general(x, up, NT, preferred_element_type=F32)
    row = jnp.arange(rows.shape[1] - model_width, dtype=jnp.int32)[:, None]
    expert = first[0] + jnp.arange(units, dtype=jnp.int32)[None, :] // width
    spread = (row % expert_total == expert).astype(BF16)
    weight = jnp.dot(rows[:, model_width:], spread, preferred_element_type=F32)
    hidden = (jax.nn.silu(gate_acts) * up_acts * weight).astype(BF16)
    return jnp.dot(hidden, down, preferred_element_type=F32).astype(BF16)


def local(tokens, expert_ids, gate_scores, gate_weight, up_weight, down_weight):
    model_width = tokens.shape[1]
    ep_count = lax.axis_size("ep")
    dp_count = lax.axis_size("dp")
    local_experts, _, width = gate_weight.shape
    expert_total = local_experts * ep_count
    gate = jnp.swapaxes(gate_weight, 1, 2).reshape(local_experts * width, model_width)
    up = jnp.swapaxes(up_weight, 1, 2).reshape(local_experts * width, model_width)
    down = down_weight.reshape(local_experts * width, model_width)
    first = (lax.axis_index("ep") * local_experts).astype(jnp.int32).reshape(1)

    sent = message(tokens, expert_ids, gate_scores, expert_total)

    powers = all(n & (n - 1) == 0 for n in (ep_count, dp_count))
    if powers and 2 <= ep_count <= 8 and 2 <= dp_count <= 8 and local_experts % 2 == 0:
        rows = gather_rows(sent, ep_count, dp_count)
        partial = experts(rows, gate, up, down, first, width, expert_total)
        return scatter_rows(partial, ep_count, dp_count)
    rows = lax.all_gather(sent, ("ep", "dp"), axis=0, tiled=True)
    partial = experts_plain(rows, gate, up, down, first, width, expert_total)
    return lax.psum_scatter(partial, ("ep", "dp"), scatter_dimension=0, tiled=True)


def solution(mesh):
    in_specs = (
        P(("rep", "ep", "dp"), None),
        P(("rep", "ep", "dp"), None),
        P(("rep", "ep", "dp"), None),
        P("ep", None, "dp"),
        P("ep", None, "dp"),
        P("ep", "dp", None),
    )
    out_specs = P(("rep", "ep", "dp"), None)
    return jax.shard_map(local, mesh=mesh, in_specs=in_specs, out_specs=out_specs, check_vma=False)
```
